32 devices in a mesh: member: 4 (over y, x), band: 8 (over z, core).
Axes of the slice: x: 2, y: 2, z: 4, core: 2. Of those that a mesh axis runs over, the one named last changes fastest.
Arguments:
- perturb: bfloat16 [80, 2, 16, 65536], P('member', None, None, 'band'), may hold values from -15 to 15
- control: float32 [2, 16, 65536], P(None, None, 'band'), may hold values from -6 to 6
- static_cov: float32 [2, 16, 16], replicated, may hold values from -1.5 to 1.5
- loc_table: bfloat16 [16, 256, 256], replicated, may hold values from -0.109375 to 0.109375
- pair_offset: int32 [256, 12], P('band'), may hold values from -6 to 6, as said below
- pair_table: int32 [256, 12], P('band'), may hold values from 0 to 15
- pair_count: int32 [256], P('band'), may hold values from 1 to 12, as said below
Outputs:
- increment: float32 [2, 16, 65536], P(None, 'member', 'band')
The draws below stay inside these ranges and needn't reach their ends.
Inputs may be any that keep to these rules, and one draw needn't show every extreme that they name: `pair_offset`: the offsets of one block are distinct. `pair_count`: counting blocks in aligned runs of 32, the first 6 and the last 6 blocks of every run have all 12 slots live; so do all blocks of some runs, the first run among them.
All inputs are finite; a program needn't handle non-finite values.
Results may differ from the reference program's by a relative error of at most 0.0022.
Values may be sent and summed in bfloat16 or wider, within the bound.
A program may use at most 128 MiB of HBM per device.

```python
import jax
import jax.numpy as jnp
from jax import lax

K = 80
F = 2
LEV = 16
COLS = 256
BLK_DEV = 32
HB = 6
PMAX = 12
NTAB = 16
NB = 256
NCOL = 65536


def draw_pair_offset(key, part):
    key = jax.random.fold_in(key, 11)
    width = 2 * HB + 1
    scores = jax.random.randint(key, (NB, width), 0, 1 << 20) * width + jnp.arange(width, dtype=jnp.int32)[None, :]
    order = jnp.argsort(scores, axis=1, stable=True)
    return (order[:, :PMAX] - HB).astype(jnp.int32)


def draw_pair_count(key, part):
    key = jax.random.fold_in(key, 23)
    first, second = jax.random.split(key)
    base = jax.random.randint(first, (NB,), 1, PMAX + 1)
    busy = jax.random.randint(second, (NB // BLK_DEV,), 0, 4) == 0
    busy = busy.at[0].set(True)
    busy = jnp.repeat(busy, BLK_DEV)
    inner = jnp.arange(NB, dtype=jnp.int32) % BLK_DEV
    edge = (inner < HB) | (inner >= BLK_DEV - HB)
    return jnp.where(busy | edge, PMAX, base).astype(jnp.int32)


def with_ends(entries, own_key, low, largest):
    index_at = [jax.random.randint(jax.random.fold_in(own_key, axis), (), 0, length) for axis, length in enumerate(entries.shape)]
    longest = entries.shape.index(max(entries.shape))
    beside = index_at[:longest] + [(index_at[longest] + 1) % entries.shape[longest]] + index_at[longest + 1:]
    return entries.at[tuple(index_at)].set(low).at[tuple(beside)].set(largest)


def steps_of(key, extent, cuts, low, high):
    def one(dim, blocks):
        steps = jax.random.uniform(jax.random.fold_in(jax.random.fold_in(key, 6), dim), (blocks,), jnp.float32, low / len(cuts), high / len(cuts))
        return jnp.repeat(jnp.exp(steps), extent[dim] // blocks).reshape((-1,) + (1,) * (len(extent) - dim - 1))

    factor_of = one(*cuts[0])
    for cut in cuts[1:]:
        factor_of = factor_of * one(*cut)
    return factor_of


def scatter_about(stream_key, shape, scale, bound, pieces=(), kind=jnp.bfloat16):
    entries = jax.random.normal(stream_key, shape, jnp.float32) * scale
    if len(pieces) > 0:
        entries = steps_of(stream_key, shape, pieces, -0.22, 0.18) * entries
    return jnp.clip(entries, min=-bound, max=bound).astype(kind)


def setup_inputs(seed: int = 0) -> dict:
    arg_keys = jax.random.split(jax.random.key(seed), 8)
    return {
        "perturb": scatter_about(arg_keys[0], (K, F, LEV, NCOL), 3.0, 15.0, ((0, 4), (3, 8))),
        "control": scatter_about(arg_keys[1], (F, LEV, NCOL), 1.0, 6.0, ((2, 8),), jnp.float32),
        "static_cov": scatter_about(arg_keys[2], (F, LEV, LEV), LEV ** -0.5, 1.5, (), jnp.float32),
        "loc_table": scatter_about(arg_keys[3], (NTAB, COLS, COLS), (COLS * PMAX) ** -0.5, 0.109375),
        "pair_offset": draw_pair_offset(jax.random.fold_in(arg_keys[7], 71), 0),
        "pair_table": with_ends(jax.random.randint(arg_keys[5], (NB, PMAX), 0, NTAB), jax.random.fold_in(arg_keys[5], 1), 0, NTAB - 1).astype(jnp.int32),
        "pair_count": draw_pair_count(jax.random.fold_in(arg_keys[7], 71), 0),
    }


def reference(perturb, control, static_cov, loc_table, pair_offset, pair_table, pair_count):
    nblk = NCOL // COLS
    rows = K * F * LEV
    words = (perturb.astype(jnp.float32) * control[None]).astype(jnp.bfloat16)
    blocks = words.reshape(rows, nblk, COLS)
    slots = jnp.arange(PMAX).astype(jnp.int32)

    def one_block(index):
        partner = ((index + pair_offset[index]) % nblk).astype(jnp.int32)
        picked = blocks[:, partner, :].astype(jnp.float32)
        tables = loc_table[pair_table[index]].astype(jnp.float32)
        prod = jnp.einsum("rpi,pij->rpj", picked, tables)
        live = (slots < pair_count[index]).astype(jnp.float32)
        return jnp.einsum("rpj,p->rj", prod, live)

    spread = lax.map(one_block, jnp.arange(nblk).astype(jnp.int32))
    spread = jnp.transpose(spread, (1, 0, 2)).reshape(K, F, LEV, NCOL)
    ensemble = jnp.sum(perturb.astype(jnp.float32) * spread, axis=0) / (K - 1)
    static = jnp.einsum("fml,flc->fmc", static_cov, control, precision=lax.Precision.HIGHEST)
    return 0.5 * static + 0.5 * ensemble
```

```python
import functools

import jax
import jax.numpy as jnp
from jax import lax
from jax.experimental import pallas as pl
from jax.experimental.pallas import tpu as pltpu
from jax.sharding import PartitionSpec as P

HB = 6
HALF = HB // 2
MESH = pl.DeviceIdType.MESH


def kernel(
    groups, bands, nblk, size, nslots, fields, levels, ntab, scale,
    info_s, info_h, perturb_h, control_h, table_h, cov_ref,
    out_ref,
    own, halo, words, tables, ctl, ctl_halo, info_halo, info_side,
    part_in, recv_in, part_edge, recv_edge, away, back,
    own_sem, misc_sem, side_sem, hsend, hrecv, asend, arecv, rsend, rrecv,
):
    rows = perturb_h.shape[0]
    depth = fields * levels
    share = levels // groups
    last = nblk + 2 * HALF
    me = lax.axis_index("member")
    mine = lax.axis_index("band")
    right = lax.rem(mine + 1, bands)
    left = lax.rem(mine + bands - 1, bands)

    barrier = pltpu.get_barrier_semaphore()
    for there in (left, right):
        pl.semaphore_signal(barrier, inc=1, device_id={"band": there}, device_id_type=MESH)
    for d in range(1, groups):
        pl.semaphore_signal(
            barrier, inc=1, device_id={"member": lax.rem(me + d, groups)}, device_id_type=MESH
        )

    def load(b):
        return pltpu.make_async_copy(
            perturb_h.at[:, pl.ds(pl.multiple_of(b * size, size), size)], own.at[b], own_sem.at[b]
        )

    def start_load(b, carry):
        load(b).start()
        return carry

    loads = [
        pltpu.make_async_copy(control_h, ctl, misc_sem.at[0]),
        pltpu.make_async_copy(table_h, tables.at[pl.ds(0, ntab)], misc_sem.at[1]),
    ]
    for copy in loads:
        copy.start()
    lax.fori_loop(0, nblk, start_load, 0)
    pl.semaphore_wait(barrier, 2 + groups - 1)

    halo_copies = []
    for side, there, first, row in ((0, right, nblk - HALF, nblk - 8), (1, left, 0, 0)):
        for n, (src, dst) in enumerate(
            [
                (info_h.at[pl.ds(row, 8)], info_halo.at[side]),
                (control_h.at[:, pl.ds(first * size, HALF * size)], ctl_halo.at[side]),
            ]
            + [
                (perturb_h.at[:, pl.ds((first + i) * size, size)], halo.at[side, i])
                for i in range(HALF)
            ]
        ):
            halo_copies.append(
                pltpu.make_async_remote_copy(
                    src_ref=src, dst_ref=dst, send_sem=hsend.at[side, n], recv_sem=hrecv.at[side, n],
                    device_id={"band": there}, device_id_type=MESH,
                )
            )
    for copy in halo_copies:
        copy.start()

    def word_of(block, weights):
        cells = block.astype(jnp.float32).reshape(rows // depth, depth, size) * weights[None]
        return cells.astype(jnp.bfloat16).reshape(rows, size)

    tables[ntab] = jnp.zeros((size, size), jnp.bfloat16)
    for i in range(HALF):
        words[i] = jnp.zeros((rows, size), jnp.bfloat16)
        words[nblk + HALF + i] = jnp.zeros((rows, size), jnp.bfloat16)
    for copy in loads:
        copy.wait()

    def make_words(b, carry):
        load(b).wait()
        words[b + HALF] = word_of(own[b], ctl[:, pl.ds(pl.multiple_of(b * size, size), size)])
        return carry

    lax.fori_loop(0, nblk, make_words, 0)

    def localize(cells, picks):
        lhs = jnp.concatenate([words[c] for c, _ in picks], axis=1)
        rhs = jnp.concatenate([tables[t] for _, t in picks], axis=0)
        spread = jnp.dot(lhs, rhs, preferred_element_type=jnp.float32)
        terms = cells.astype(jnp.float32) * spread
        return jnp.sum(terms.reshape(rows // depth, depth, size), axis=0)

    def put(dst, total):
        for m in range(groups):
            for f in range(fields):
                at = f * levels + m * share
                dst(m, slice(f * share, (f + 1) * share), total[at:at + share])

    def interior(n, carry):
        b = n + HB
        picks = [
            (b + HALF + info_s[b, s], info_s[b, nslots + s]) for s in range(nslots)
        ]
        cols = pl.ds(pl.multiple_of(n * size, size), size)

        def dst(m, at, value):
            part_in[m, at, cols] = value

        put(dst, localize(own[b], picks))
        return carry

    lax.fori_loop(0, nblk - 2 * HB, interior, 0)

    def to_members(src, dst, n):
        copies = []
        for d in range(1, groups):
            there = lax.rem(me + d, groups)
            copies.append(
                pltpu.make_async_remote_copy(
                    src_ref=src.at[there], dst_ref=dst.at[d - 1],
                    send_sem=rsend.at[n, d - 1], recv_sem=rrecv.at[n, d - 1],
                    device_id={"member": there}, device_id_type=MESH,
                )
            )
        for copy in copies:
            copy.start()
        return copies

    sums = to_members(part_in, recv_in, 0)

    out_ref[...] = 0.5 * jnp.dot(
        cov_ref[...], ctl[...], precision=lax.Precision.HIGHEST, preferred_element_type=jnp.float32
    )

    for copy in halo_copies:
        copy.wait()
    sides = [
        pltpu.make_async_copy(info_halo.at[side], info_side.at[side], side_sem.at[side])
        for side in range(2)
    ]
    for copy in sides:
        copy.start()
    for side in range(2):
        for i in range(HALF):
            words[side * (nblk + HALF) + i] = word_of(
                halo[side, i], ctl_halo[side, :, i * size:(i + 1) * size]
            )
    for copy in sides:
        copy.wait()

    for side in range(2):
        for i in range(HALF):
            row = 8 - HALF + i if side == 0 else i
            b = i if side == 0 else nblk + HALF + i
            partners = range(2 * HALF, 2 * HALF + i + 1) if side == 0 else range(
                b - HB, nblk
            )
            picks = []
            for c in partners:
                t = jnp.int32(ntab)
                for s in range(nslots):
                    hit = info_side[side, row, s] == c - b
                    t = jnp.where(hit, info_side[side, row, nslots + s], t)
                picks.append((c, t))
            total = localize(halo[side, i], picks)

            def dst(m, at, value):
                away[side, m, at, i * size:(i + 1) * size] = value

            put(dst, total)
    away_copies = [
        pltpu.make_async_remote_copy(
            src_ref=away.at[side], dst_ref=back.at[1 - side],
            send_sem=asend.at[side], recv_sem=arecv.at[side],
            device_id={"band": there}, device_id_type=MESH,
        )
        for side, there in ((0, left), (1, right))
    ]
    for copy in away_copies:
        copy.start()

    for side in range(2):
        def edge(n, carry):
            b = n + side * (nblk - HB)
            picks = []
            for s in range(nslots):
                c = b + HALF + info_s[b, s]
                held = (c >= 0) & (c < last)
                picks.append(
                    (jnp.clip(c, 0, last - 1), jnp.where(held, info_s[b, nslots + s], ntab))
                )
            cols = pl.ds(pl.multiple_of(n * size, size), size)

            def dst(m, at, value):
                part_edge[side, m, at, cols] = value

            put(dst, localize(own[b], picks))
            return carry

        lax.fori_loop(0, HB, edge, 0)
        if side == 0:
            for copy in away_copies:
                copy.wait()
        near = pl.ds(side * HALF * size, HALF * size)
        part_edge[side, :, :, near] = part_edge[side, :, :, near] + back[side]
        sums = sums + to_members(part_edge.at[side], recv_edge.at[side], 1 + side)

    for copy in sums:
        copy.wait()

    def finish(first, width, own_part, others):
        total = own_part
        for d in range(groups - 1):
            total = total + others[d]
        cols = slice(first * size, (first + width) * size)
        out_ref[:, cols] = out_ref[:, cols] + 0.5 * (total / scale)

    finish(HB, nblk - 2 * HB, part_in[me], recv_in)
    for side in range(2):
        finish(side * (nblk - HB), HB, part_edge[side, me], recv_edge.at[side])


def per_device(perturb, control, static_cov, loc_table, pair_offset, pair_table, pair_count):
    groups = lax.axis_size("member")
    bands = lax.axis_size("band")
    members, fields, levels, width = perturb.shape
    ntab, size = loc_table.shape[:2]
    nblk, nslots = pair_offset.shape
    share = levels // groups
    rows = members * fields * levels
    depth = fields * levels

    live = jnp.arange(nslots, dtype=jnp.int32)[None, :] < pair_count[:, None]
    info = jnp.concatenate(
        [jnp.where(live, pair_offset, 0), jnp.where(live, pair_table, ntab)], axis=1
    )
    info = jnp.pad(info, ((0, 0), (0, 128 - 2 * nslots)))
    first = lax.axis_index("member") * share
    cov_mine = lax.dynamic_slice_in_dim(static_cov, first, share, 1)
    cov = (cov_mine[:, :, None, :] * jnp.eye(fields, dtype=jnp.float32)[:, None, :, None]).reshape(
        fields * share, depth
    )

    out_rows = fields * share
    f32, bf16 = jnp.float32, jnp.bfloat16
    any_spec = pl.BlockSpec(memory_space=pl.ANY)
    dma = pltpu.SemaphoreType.DMA
    pairs = nblk * nslots
    out = pl.pallas_call(
        functools.partial(
            kernel, groups, bands, nblk, size, nslots, fields, levels, ntab, members * groups - 1
        ),
        out_shape=jax.ShapeDtypeStruct((out_rows, width), f32),
        in_specs=[
            pl.BlockSpec(memory_space=pltpu.SMEM), any_spec, any_spec, any_spec, any_spec,
            pl.BlockSpec(memory_space=pltpu.VMEM),
        ],
        out_specs=pl.BlockSpec(memory_space=pltpu.VMEM),
        scratch_shapes=[
            pltpu.VMEM((nblk, rows, size), bf16),
            pltpu.VMEM((2, HALF, rows, size), bf16),
            pltpu.VMEM((nblk + 2 * HALF, rows, size), bf16),
            pltpu.VMEM((ntab + 1, size, size), bf16),
            pltpu.VMEM((depth, width), f32),
            pltpu.VMEM((2, depth, HALF * size), f32),
            pltpu.VMEM((2, 8, 128), jnp.int32),
            pltpu.SMEM((2, 8, 128), jnp.int32),
            pltpu.VMEM((groups, out_rows, width - 2 * HB * size), f32),
            pltpu.VMEM((groups - 1, out_rows, width - 2 * HB * size), f32),
            pltpu.VMEM((2, groups, out_rows, HB * size), f32),
            pltpu.VMEM((2, groups - 1, out_rows, HB * size), f32),
            pltpu.VMEM((2, groups, out_rows, HALF * size), f32),
            pltpu.VMEM((2, groups, out_rows, HALF * size), f32),
            dma((nblk,)), dma((2,)), dma((2,)),
            dma((2, 2 + HALF)), dma((2, 2 + HALF)),
            dma((2,)), dma((2,)),
            dma((3, groups - 1)), dma((3, groups - 1)),
        ],
        compiler_params=pltpu.CompilerParams(
            collective_id=0, has_side_effects=True, vmem_limit_bytes=56 * 1024 * 1024
        ),
        cost_estimate=pl.CostEstimate(
            flops=2 * pairs * rows * size * size, bytes_accessed=2 * rows * width, transcendentals=0
        ),
    )(info, info, perturb.reshape(rows, width), control.reshape(depth, width), loc_table, cov)
    return out.reshape(fields, share, width)


def solution(mesh):
    return jax.shard_map(
        per_device,
        mesh=mesh,
        in_specs=(
            P("member", None, None, "band"),
            P(None, None, "band"),
            P(),
            P(),
            P("band", None),
            P("band", None),
            P("band"),
        ),
        out_specs=P(None, "member", "band"),
        check_vma=False,
    )
```

```python
import functools

import jax
import jax.numpy as jnp
from jax import lax
from jax.experimental import pallas as pl
from jax.experimental.pallas import tpu as pltpu
from jax.sharding import PartitionSpec as P

HB = 6
HALF = HB // 2
MESH = pl.DeviceIdType.MESH


def kernel(
    groups, bands, nblk, size, nslots, fields, levels, ntab, scale,
    off_s, tab_s, cnt_s, off_h, tab_h, cnt_h, perturb_h, control_h, table_h, cov_ref,
    out_ref,
    own, halo, words, tables, ctl, ctl_halo,
    off_halo, tab_halo, cnt_halo, off_side, tab_side, cnt_side,
    part_in, recv_in, part_edge, recv_edge, away, back,
    own_sem, misc_sem, side_sem, hsend, hrecv, asend, arecv, rsend, rrecv,
):
    rows = perturb_h.shape[0]
    depth = fields * levels
    share = levels // groups
    last = nblk + 2 * HALF
    me = lax.axis_index("member")
    mine = lax.axis_index("band")
    right = lax.rem(mine + 1, bands)
    left = lax.rem(mine + bands - 1, bands)

    barrier = pltpu.get_barrier_semaphore()
    for there in (left, right):
        pl.semaphore_signal(barrier, inc=1, device_id={"band": there}, device_id_type=MESH)
    for d in range(1, groups):
        pl.semaphore_signal(
            barrier, inc=1, device_id={"member": lax.rem(me + d, groups)}, device_id_type=MESH
        )

    def load(b):
        return pltpu.make_async_copy(
            perturb_h.at[:, pl.ds(pl.multiple_of(b * size, size), size)], own.at[b], own_sem.at[b]
        )

    def start_load(b, carry):
        load(b).start()
        return carry

    loads = [
        pltpu.make_async_copy(control_h, ctl, misc_sem.at[0]),
        pltpu.make_async_copy(table_h, tables.at[pl.ds(0, ntab)], misc_sem.at[1]),
    ]
    for copy in loads:
        copy.start()
    lax.fori_loop(0, nblk, start_load, 0)
    pl.semaphore_wait(barrier, 2 + groups - 1)

    halo_copies = []
    for side, there, first in ((0, right, nblk - HALF), (1, left, 0)):
        for n, (src, dst) in enumerate(
            [
                (off_h, off_halo.at[side]),
                (tab_h, tab_halo.at[side]),
                (cnt_h, cnt_halo.at[side]),
                (control_h.at[:, pl.ds(first * size, HALF * size)], ctl_halo.at[side]),
            ]
            + [
                (perturb_h.at[:, pl.ds((first + i) * size, size)], halo.at[side, i])
                for i in range(HALF)
            ]
        ):
            halo_copies.append(
                pltpu.make_async_remote_copy(
                    src_ref=src, dst_ref=dst, send_sem=hsend.at[side, n], recv_sem=hrecv.at[side, n],
                    device_id={"band": there}, device_id_type=MESH,
                )
            )
    for copy in halo_copies:
        copy.start()

    def word_of(block, weights):
        cells = block.astype(jnp.float32).reshape(rows // depth, depth, size) * weights[None]
        return cells.astype(jnp.bfloat16).reshape(rows, size)

    tables[ntab] = jnp.zeros((size, size), jnp.bfloat16)
    for i in range(HALF):
        words[i] = jnp.zeros((rows, size), jnp.bfloat16)
        words[nblk + HALF + i] = jnp.zeros((rows, size), jnp.bfloat16)
    for copy in loads:
        copy.wait()

    def make_words(b, carry):
        load(b).wait()
        words[b + HALF] = word_of(own[b], ctl[:, pl.ds(pl.multiple_of(b * size, size), size)])
        return carry

    lax.fori_loop(0, nblk, make_words, 0)

    def localize(cells, picks):
        spread = None
        for c, t in picks:
            term = jnp.dot(words[c], tables[t], preferred_element_type=jnp.float32)
            spread = term if spread is None else spread + term
        terms = cells.astype(jnp.float32) * spread
        return jnp.sum(terms.reshape(rows // depth, depth, size), axis=0)

    def put(dst, total):
        for m in range(groups):
            for f in range(fields):
                at = f * levels + m * share
                dst(m, slice(f * share, (f + 1) * share), total[at:at + share])

    def interior(n, carry):
        b = n + HB
        picks = [
            (b + HALF + off_s[s, b], jnp.where(s < cnt_s[0, b], tab_s[s, b], ntab))
            for s in range(nslots)
        ]
        cols = pl.ds(pl.multiple_of(n * size, size), size)

        def dst(m, at, value):
            part_in[m, at, cols] = value

        put(dst, localize(own[b], picks))
        return carry

    lax.fori_loop(0, nblk - 2 * HB, interior, 0)

    def to_members(src, dst, n):
        copies = []
        for d in range(1, groups):
            there = lax.rem(me + d, groups)
            copies.append(
                pltpu.make_async_remote_copy(
                    src_ref=src.at[there], dst_ref=dst.at[d - 1],
                    send_sem=rsend.at[n, d - 1], recv_sem=rrecv.at[n, d - 1],
                    device_id={"member": there}, device_id_type=MESH,
                )
            )
        for copy in copies:
            copy.start()
        return copies

    sums = [to_members(part_in, recv_in, 0)]

    chunk = 4 * size

    def static(n, carry):
        cols = pl.ds(pl.multiple_of(n * chunk, chunk), chunk)
        for f in range(fields):
            cov = cov_ref[f, 0:share]
            for m in range(1, groups):
                cov = jnp.where(me == m, cov_ref[f, m * share:(m + 1) * share], cov)
            total = cov[:, 0:1] * ctl[f * levels:f * levels + 1, cols]
            for l in range(1, levels):
                at = f * levels + l
                total = total + cov[:, l:l + 1] * ctl[at:at + 1, cols]
            out_ref[f, :, cols] = 0.5 * total
        return carry

    lax.fori_loop(0, nblk * size // chunk, static, 0)

    for copy in halo_copies:
        copy.wait()
    sides = [
        pltpu.make_async_copy(src.at[side], dst.at[side], side_sem.at[side, n])
        for side in range(2)
        for n, (src, dst) in enumerate(
            [(off_halo, off_side), (tab_halo, tab_side), (cnt_halo, cnt_side)]
        )
    ]
    for copy in sides:
        copy.start()
    for side in range(2):
        for i in range(HALF):
            words[side * (nblk + HALF) + i] = word_of(
                halo[side, i], ctl_halo[side, :, i * size:(i + 1) * size]
            )
    for copy in sides:
        copy.wait()

    for side in range(2):
        for i in range(HALF):
            there = nblk - HALF + i if side == 0 else i
            b = i if side == 0 else nblk + HALF + i
            partners = range(2 * HALF, 2 * HALF + i + 1) if side == 0 else range(
                b - HB, nblk
            )
            picks = []
            for c in partners:
                t = jnp.int32(ntab)
                for s in range(nslots):
                    hit = (off_side[side, s, there] == c - b) & (s < cnt_side[side, 0, there])
                    t = jnp.where(hit, tab_side[side, s, there], t)
                picks.append((c, t))
            total = localize(halo[side, i], picks)

            def dst(m, at, value):
                away[side, m, at, i * size:(i + 1) * size] = value

            put(dst, total)
    away_copies = [
        pltpu.make_async_remote_copy(
            src_ref=away.at[side], dst_ref=back.at[1 - side],
            send_sem=asend.at[side], recv_sem=arecv.at[side],
            device_id={"band": there}, device_id_type=MESH,
        )
        for side, there in ((0, left), (1, right))
    ]
    for copy in away_copies:
        copy.start()

    for side in range(2):
        def edge(n, carry):
            b = n + side * (nblk - HB)
            picks = []
            for s in range(nslots):
                c = b + HALF + off_s[s, b]
                held = (c >= 0) & (c < last) & (s < cnt_s[0, b])
                picks.append((jnp.clip(c, 0, last - 1), jnp.where(held, tab_s[s, b], ntab)))
            cols = pl.ds(pl.multiple_of(n * size, size), size)

            def dst(m, at, value):
                part_edge[side, m, at, cols] = value

            put(dst, localize(own[b], picks))
            return carry

        lax.fori_loop(0, HB, edge, 0)
        if side == 0:
            for copy in away_copies:
                copy.wait()
        near = pl.ds(side * HALF * size, HALF * size)
        part_edge[side, :, :, near] = part_edge[side, :, :, near] + back[side]
        sums.append(to_members(part_edge.at[side], recv_edge.at[side], 1 + side))

    def finish(copies, first, width, own_part, others):
        for copy in copies:
            copy.wait()
        total = own_part
        for d in range(groups - 1):
            total = total + others[d]
        cols = slice(first * size, (first + width) * size)
        for f in range(fields):
            out_ref[f, :, cols] = out_ref[f, :, cols] + 0.5 * (
                total[f * share:(f + 1) * share] / scale
            )

    finish(sums[0], HB, nblk - 2 * HB, part_in[me], recv_in)
    for side in range(2):
        finish(sums[1 + side], side * (nblk - HB), HB, part_edge[side, me], recv_edge.at[side])


def per_device(perturb, control, static_cov, loc_table, pair_offset, pair_table, pair_count):
    groups = lax.axis_size("member")
    bands = lax.axis_size("band")
    members, fields, levels, width = perturb.shape
    ntab, size = loc_table.shape[:2]
    nblk, nslots = pair_offset.shape
    share = levels // groups
    rows = members * fields * levels
    depth = fields * levels

    offsets = pair_offset.T
    table_ids = pair_table.T
    counts = pair_count.reshape(1, nblk)
    out_rows = fields * share
    f32, bf16, i32 = jnp.float32, jnp.bfloat16, jnp.int32
    smem = pl.BlockSpec(memory_space=pltpu.SMEM)
    any_spec = pl.BlockSpec(memory_space=pl.ANY)
    dma = pltpu.SemaphoreType.DMA
    pairs = nblk * nslots
    return pl.pallas_call(
        functools.partial(
            kernel, groups, bands, nblk, size, nslots, fields, levels, ntab, members * groups - 1
        ),
        out_shape=jax.ShapeDtypeStruct((fields, share, width), f32),
        in_specs=[
            smem, smem, smem, any_spec, any_spec, any_spec, any_spec, any_spec, any_spec,
            pl.BlockSpec(memory_space=pltpu.VMEM),
        ],
        out_specs=pl.BlockSpec(memory_space=pltpu.VMEM),
        scratch_shapes=[
            pltpu.VMEM((nblk, rows, size), bf16),
            pltpu.VMEM((2, HALF, rows, size), bf16),
            pltpu.VMEM((nblk + 2 * HALF, rows, size), bf16),
            pltpu.VMEM((ntab + 1, size, size), bf16),
            pltpu.VMEM((depth, width), f32),
            pltpu.VMEM((2, depth, HALF * size), f32),
            pltpu.VMEM((2, nslots, nblk), i32),
            pltpu.VMEM((2, nslots, nblk), i32),
            pltpu.VMEM((2, 1, nblk), i32),
            pltpu.SMEM((2, nslots, nblk), i32),
            pltpu.SMEM((2, nslots, nblk), i32),
            pltpu.SMEM((2, 1, nblk), i32),
            pltpu.VMEM((groups, out_rows, width - 2 * HB * size), f32),
            pltpu.VMEM((groups - 1, out_rows, width - 2 * HB * size), f32),
            pltpu.VMEM((2, groups, out_rows, HB * size), f32),
            pltpu.VMEM((2, groups - 1, out_rows, HB * size), f32),
            pltpu.VMEM((2, groups, out_rows, HALF * size), f32),
            pltpu.VMEM((2, groups, out_rows, HALF * size), f32),
            dma((nblk,)), dma((2,)), dma((2, 3)),
            dma((2, 4 + HALF)), dma((2, 4 + HALF)),
            dma((2,)), dma((2,)),
            dma((3, groups - 1)), dma((3, groups - 1)),
        ],
        compiler_params=pltpu.CompilerParams(
            collective_id=0, has_side_effects=True, vmem_limit_bytes=56 * 1024 * 1024
        ),
        cost_estimate=pl.CostEstimate(
            flops=2 * pairs * rows * size * size, bytes_accessed=2 * rows * width, transcendentals=0
        ),
    )(
        offsets, table_ids, counts, offsets, table_ids, counts,
        perturb.reshape(rows, width), control.reshape(depth, width), loc_table, static_cov,
    )


def solution(mesh):
    return jax.shard_map(
        per_device,
        mesh=mesh,
        in_specs=(
            P("member", None, None, "band"),
            P(None, None, "band"),
            P(),
            P(),
            P("band", None),
            P("band", None),
            P("band"),
        ),
        out_specs=P(None, "member", "band"),
        check_vma=False,
    )
```

```python
import functools

import jax
import jax.numpy as jnp
from jax import lax
from jax.experimental import pallas as pl
from jax.experimental.pallas import tpu as pltpu
from jax.sharding import PartitionSpec as P

HB = 6
HALF = HB // 2
GROUP = 5
MESH = pl.DeviceIdType.MESH


def kernel(
    groups, bands, nblk, size, nslots, fields, levels, ntab, scale,
    off_s, tab_s, cnt_s, off_h, tab_h, cnt_h, perturb_h, control_h, table_h, cov_ref,
    out_ref,
    own, halo, words, tables, ctl, ctl_halo,
    off_halo, tab_halo, cnt_halo, off_side, tab_side, cnt_side,
    part_in, recv_in, part_edge, recv_edge, away, back,
    own_sem, misc_sem, side_sem, hsend, hrecv, asend, arecv, rsend, rrecv,
):
    rows = perturb_h.shape[0]
    depth = fields * levels
    share = levels // groups
    last = nblk + 2 * HALF
    me = lax.axis_index("member")
    mine = lax.axis_index("band")
    right = lax.rem(mine + 1, bands)
    left = lax.rem(mine + bands - 1, bands)

    barrier = pltpu.get_barrier_semaphore()
    for there in (left, right):
        pl.semaphore_signal(barrier, inc=1, device_id={"band": there}, device_id_type=MESH)
    for d in range(1, groups):
        pl.semaphore_signal(
            barrier, inc=1, device_id={"member": lax.rem(me + d, groups)}, device_id_type=MESH
        )

    def load(b):
        return pltpu.make_async_copy(
            perturb_h.at[:, pl.ds(pl.multiple_of(b * size, size), size)], own.at[b], own_sem.at[b]
        )

    def start_load(b, carry):
        load(b).start()
        return carry

    loads = [
        pltpu.make_async_copy(control_h, ctl, misc_sem.at[0]),
        pltpu.make_async_copy(table_h, tables.at[pl.ds(0, ntab)], misc_sem.at[1]),
    ]
    for copy in loads:
        copy.start()
    lax.fori_loop(0, nblk, start_load, 0)
    pl.semaphore_wait(barrier, 2 + groups - 1)

    halo_copies = []
    for side, there, first in ((0, right, nblk - HALF), (1, left, 0)):
        for n, (src, dst) in enumerate(
            [
                (off_h, off_halo.at[side]),
                (tab_h, tab_halo.at[side]),
                (cnt_h, cnt_halo.at[side]),
                (control_h.at[:, pl.ds(first * size, HALF * size)], ctl_halo.at[side]),
            ]
            + [
                (perturb_h.at[:, pl.ds((first + i) * size, size)], halo.at[side, i])
                for i in range(HALF)
            ]
        ):
            halo_copies.append(
                pltpu.make_async_remote_copy(
                    src_ref=src, dst_ref=dst, send_sem=hsend.at[side, n], recv_sem=hrecv.at[side, n],
                    device_id={"band": there}, device_id_type=MESH,
                )
            )
    for copy in halo_copies:
        copy.start()

    def word_of(block, weights):
        cells = block.astype(jnp.float32).reshape(rows // depth, depth, size) * weights[None]
        return cells.astype(jnp.bfloat16).reshape(rows, size)

    tables[ntab] = jnp.zeros((size, size), jnp.bfloat16)
    for i in range(HALF):
        words[i] = jnp.zeros((rows, size), jnp.bfloat16)
        words[nblk + HALF + i] = jnp.zeros((rows, size), jnp.bfloat16)
    for copy in loads:
        copy.wait()

    def make_words(b, carry):
        load(b).wait()
        words[b + HALF] = word_of(own[b], ctl[:, pl.ds(pl.multiple_of(b * size, size), size)])
        return carry

    lax.fori_loop(0, nblk, make_words, 0)

    members = rows // depth
    group = max(g for g in range(1, GROUP + 1) if members % g == 0)

    def localize(cells, picks):
        total = None
        for first in range(0, rows, group * depth):
            at = pl.ds(first, group * depth)
            spread = None
            for c, t in picks:
                term = jnp.dot(words[c, at], tables[t], preferred_element_type=jnp.float32)
                spread = term if spread is None else spread + term
            terms = cells[at].astype(jnp.float32) * spread
            part = jnp.sum(terms.reshape(group, depth, size), axis=0)
            total = part if total is None else total + part
        return total

    def put(dst, total):
        for m in range(groups):
            for f in range(fields):
                at = f * levels + m * share
                dst(m, slice(f * share, (f + 1) * share), total[at:at + share])

    def interior(n, carry):
        b = n + HB
        picks = [
            (b + HALF + off_s[s, b], jnp.where(s < cnt_s[0, b], tab_s[s, b], ntab))
            for s in range(nslots)
        ]
        cols = pl.ds(pl.multiple_of(n * size, size), size)

        def dst(m, at, value):
            part_in[m, at, cols] = value

        put(dst, localize(own.at[b], picks))
        return carry

    lax.fori_loop(0, nblk - 2 * HB, interior, 0)

    def to_members(src, dst, n):
        copies = []
        for d in range(1, groups):
            there = lax.rem(me + d, groups)
            copies.append(
                pltpu.make_async_remote_copy(
                    src_ref=src.at[there], dst_ref=dst.at[d - 1],
                    send_sem=rsend.at[n, d - 1], recv_sem=rrecv.at[n, d - 1],
                    device_id={"member": there}, device_id_type=MESH,
                )
            )
        for copy in copies:
            copy.start()
        return copies

    sums = [to_members(part_in, recv_in, 0)]

    chunk = 4 * size

    def static(n, carry):
        cols = pl.ds(pl.multiple_of(n * chunk, chunk), chunk)
        for f in range(fields):
            cov = cov_ref[f, 0:share]
            for m in range(1, groups):
                cov = jnp.where(me == m, cov_ref[f, m * share:(m + 1) * share], cov)
            total = cov[:, 0:1] * ctl[f * levels:f * levels + 1, cols]
            for l in range(1, levels):
                at = f * levels + l
                total = total + cov[:, l:l + 1] * ctl[at:at + 1, cols]
            out_ref[f, :, cols] = 0.5 * total
        return carry

    lax.fori_loop(0, nblk * size // chunk, static, 0)

    for copy in halo_copies:
        copy.wait()
    sides = [
        pltpu.make_async_copy(src.at[side], dst.at[side], side_sem.at[side, n])
        for side in range(2)
        for n, (src, dst) in enumerate(
            [(off_halo, off_side), (tab_halo, tab_side), (cnt_halo, cnt_side)]
        )
    ]
    for copy in sides:
        copy.start()
    for side in range(2):
        for i in range(HALF):
            words[side * (nblk + HALF) + i] = word_of(
                halo[side, i], ctl_halo[side, :, i * size:(i + 1) * size]
            )
    for copy in sides:
        copy.wait()

    for side in range(2):
        for i in range(HALF):
            there = nblk - HALF + i if side == 0 else i
            b = i if side == 0 else nblk + HALF + i
            partners = range(2 * HALF, 2 * HALF + i + 1) if side == 0 else range(
                b - HB, nblk
            )
            picks = []
            for c in partners:
                t = jnp.int32(ntab)
                for s in range(nslots):
                    hit = (off_side[side, s, there] == c - b) & (s < cnt_side[side, 0, there])
                    t = jnp.where(hit, tab_side[side, s, there], t)
                picks.append((c, t))
            total = localize(halo.at[side, i], picks)

            def dst(m, at, value):
                away[side, m, at, i * size:(i + 1) * size] = value

            put(dst, total)
    away_copies = [
        pltpu.make_async_remote_copy(
            src_ref=away.at[side], dst_ref=back.at[1 - side],
            send_sem=asend.at[side], recv_sem=arecv.at[side],
            device_id={"band": there}, device_id_type=MESH,
        )
        for side, there in ((0, left), (1, right))
    ]
    for copy in away_copies:
        copy.start()

    for side in range(2):
        def edge(n, carry):
            b = n + side * (nblk - HB)
            picks = []
            for s in range(nslots):
                c = b + HALF + off_s[s, b]
                held = (c >= 0) & (c < last) & (s < cnt_s[0, b])
                picks.append((jnp.clip(c, 0, last - 1), jnp.where(held, tab_s[s, b], ntab)))
            cols = pl.ds(pl.multiple_of(n * size, size), size)

            def dst(m, at, value):
                part_edge[side, m, at, cols] = value

            put(dst, localize(own.at[b], picks))
            return carry

        lax.fori_loop(0, HB, edge, 0)
        if side == 0:
            for copy in away_copies:
                copy.wait()
        near = pl.ds(side * HALF * size, HALF * size)
        part_edge[side, :, :, near] = part_edge[side, :, :, near] + back[side]
        sums.append(to_members(part_edge.at[side], recv_edge.at[side], 1 + side))

    def finish(copies, first, width, own_part, others):
        for copy in copies:
            copy.wait()
        total = own_part
        for d in range(groups - 1):
            total = total + others[d]
        cols = slice(first * size, (first + width) * size)
        for f in range(fields):
            out_ref[f, :, cols] = out_ref[f, :, cols] + 0.5 * (
                total[f * share:(f + 1) * share] / scale
            )

    finish(sums[0], HB, nblk - 2 * HB, part_in[me], recv_in)
    for side in range(2):
        finish(sums[1 + side], side * (nblk - HB), HB, part_edge[side, me], recv_edge.at[side])


def per_device(perturb, control, static_cov, loc_table, pair_offset, pair_table, pair_count):
    groups = lax.axis_size("member")
    bands = lax.axis_size("band")
    members, fields, levels, width = perturb.shape
    ntab, size = loc_table.shape[:2]
    nblk, nslots = pair_offset.shape
    share = levels // groups
    rows = members * fields * levels
    depth = fields * levels

    offsets = pair_offset.T
    table_ids = pair_table.T
    counts = pair_count.reshape(1, nblk)
    out_rows = fields * share
    f32, bf16, i32 = jnp.float32, jnp.bfloat16, jnp.int32
    smem = pl.BlockSpec(memory_space=pltpu.SMEM)
    any_spec = pl.BlockSpec(memory_space=pl.ANY)
    dma = pltpu.SemaphoreType.DMA
    pairs = nblk * nslots
    return pl.pallas_call(
        functools.partial(
            kernel, groups, bands, nblk, size, nslots, fields, levels, ntab, members * groups - 1
        ),
        out_shape=jax.ShapeDtypeStruct((fields, share, width), f32),
        in_specs=[
            smem, smem, smem, any_spec, any_spec, any_spec, any_spec, any_spec, any_spec,
            pl.BlockSpec(memory_space=pltpu.VMEM),
        ],
        out_specs=pl.BlockSpec(memory_space=pltpu.VMEM),
        scratch_shapes=[
            pltpu.VMEM((nblk, rows, size), bf16),
            pltpu.VMEM((2, HALF, rows, size), bf16),
            pltpu.VMEM((nblk + 2 * HALF, rows, size), bf16),
            pltpu.VMEM((ntab + 1, size, size), bf16),
            pltpu.VMEM((depth, width), f32),
            pltpu.VMEM((2, depth, HALF * size), f32),
            pltpu.VMEM((2, nslots, nblk), i32),
            pltpu.VMEM((2, nslots, nblk), i32),
            pltpu.VMEM((2, 1, nblk), i32),
            pltpu.SMEM((2, nslots, nblk), i32),
            pltpu.SMEM((2, nslots, nblk), i32),
            pltpu.SMEM((2, 1, nblk), i32),
            pltpu.VMEM((groups, out_rows, width - 2 * HB * size), f32),
            pltpu.VMEM((groups - 1, out_rows, width - 2 * HB * size), f32),
            pltpu.VMEM((2, groups, out_rows, HB * size), f32),
            pltpu.VMEM((2, groups - 1, out_rows, HB * size), f32),
            pltpu.VMEM((2, groups, out_rows, HALF * size), f32),
            pltpu.VMEM((2, groups, out_rows, HALF * size), f32),
            dma((nblk,)), dma((2,)), dma((2, 3)),
            dma((2, 4 + HALF)), dma((2, 4 + HALF)),
            dma((2,)), dma((2,)),
            dma((3, groups - 1)), dma((3, groups - 1)),
        ],
        compiler_params=pltpu.CompilerParams(
            collective_id=0, has_side_effects=True, vmem_limit_bytes=56 * 1024 * 1024
        ),
        cost_estimate=pl.CostEstimate(
            flops=2 * pairs * rows * size * size, bytes_accessed=2 * rows * width, transcendentals=0
        ),
    )(
        offsets, table_ids, counts, offsets, table_ids, counts,
        perturb.reshape(rows, width), control.reshape(depth, width), loc_table, static_cov,
    )


def solution(mesh):
    return jax.shard_map(
        per_device,
        mesh=mesh,
        in_specs=(
            P("member", None, None, "band"),
            P(None, None, "band"),
            P(),
            P(),
            P("band", None),
            P("band", None),
            P("band"),
        ),
        out_specs=P(None, "member", "band"),
        check_vma=False,
    )
```

```python
import functools

import jax
import jax.numpy as jnp
from jax import lax
from jax.experimental import pallas as pl
from jax.experimental.pallas import tpu as pltpu
from jax.sharding import PartitionSpec as P

HB = 6
HALF = HB // 2
GROUP = 5
MESH = pl.DeviceIdType.MESH


def kernel(
    groups, bands, nblk, size, nslots, fields, levels, ntab, scale,
    off_s, tab_s, cnt_s, off_h, tab_h, cnt_h, perturb_h, control_h, table_h, cov_ref,
    out_ref,
    own, halo, words, tables, ctl, ctl_halo,
    off_halo, tab_halo, cnt_halo, off_side, tab_side, cnt_side,
    part_in, recv_in, part_edge, recv_edge, away, back,
    own_sem, misc_sem, side_sem, hsend, hrecv, asend, arecv, rsend, rrecv,
):
    rows = perturb_h.shape[0]
    depth = fields * levels
    share = levels // groups
    last = nblk + 2 * HALF
    me = lax.axis_index("member")
    mine = lax.axis_index("band")
    right = lax.rem(mine + 1, bands)
    left = lax.rem(mine + bands - 1, bands)

    barrier = pltpu.get_barrier_semaphore()
    for there in (left, right):
        pl.semaphore_signal(barrier, inc=1, device_id={"band": there}, device_id_type=MESH)
    for d in range(1, groups):
        pl.semaphore_signal(
            barrier, inc=1, device_id={"member": lax.rem(me + d, groups)}, device_id_type=MESH
        )

    ends = [*range(HALF), *range(nblk - HALF, nblk)]

    def load(b):
        return pltpu.make_async_copy(
            perturb_h.at[:, pl.ds(pl.multiple_of(b * size, size), size)], own.at[b], own_sem.at[b]
        )

    def start_load(b, carry):
        load(b).start()
        return carry

    for b in ends:
        load(b).start()
    loads = [
        pltpu.make_async_copy(control_h, ctl, misc_sem.at[0]),
        pltpu.make_async_copy(table_h, tables.at[pl.ds(0, ntab)], misc_sem.at[1]),
    ]
    for copy in loads:
        copy.start()
    lax.fori_loop(HALF, nblk - HALF, start_load, 0)

    near = lax.rem(mine + 1, 2)
    far = 1 - near

    def toward(side):
        return jnp.where(side == 0, left, right)

    def halo_copies(side):
        first = jnp.where(side == 0, 0, nblk - HALF)
        cols = pl.ds(pl.multiple_of(first * size, size), HALF * size)
        return [
            pltpu.make_async_remote_copy(
                src_ref=src, dst_ref=dst.at[1 - side],
                send_sem=hsend.at[side, n], recv_sem=hrecv.at[1 - side, n],
                device_id={"band": toward(side)}, device_id_type=MESH,
            )
            for n, (src, dst) in enumerate(
                [
                    (own.at[pl.ds(first, HALF)], halo),
                    (control_h.at[:, cols], ctl_halo),
                    (off_h, off_halo),
                    (tab_h, tab_halo),
                    (cnt_h, cnt_halo),
                ]
            )
        ]

    for b in ends:
        load(b).wait()
    pl.semaphore_wait(barrier, 2 + groups - 1)
    for side in (far, near):
        for copy in halo_copies(side):
            copy.start()

    def word_of(block, weights):
        cells = block.astype(jnp.float32).reshape(rows // depth, depth, size) * weights[None]
        return cells.astype(jnp.bfloat16).reshape(rows, size)

    tables[ntab] = jnp.zeros((size, size), jnp.bfloat16)
    for i in range(HALF):
        words[i] = jnp.zeros((rows, size), jnp.bfloat16)
        words[nblk + HALF + i] = jnp.zeros((rows, size), jnp.bfloat16)
    for copy in loads:
        copy.wait()

    def make_words(b, carry):
        words[b + HALF] = word_of(own[b], ctl[:, pl.ds(pl.multiple_of(b * size, size), size)])
        return carry

    def end_words(n, carry):
        return make_words(jnp.where(n < HALF, n, nblk - 2 * HALF + n), carry)

    def loaded_words(b, carry):
        load(b).wait()
        return make_words(b, carry)

    lax.fori_loop(0, 2 * HALF, end_words, 0)
    lax.fori_loop(HALF, nblk - HALF, loaded_words, 0)

    members = rows // depth
    group = max(g for g in range(1, GROUP + 1) if members % g == 0)

    def localize(cells, picks):
        total = None
        for first in range(0, rows, group * depth):
            at = pl.ds(first, group * depth)
            spread = None
            for c, t in picks:
                term = jnp.dot(words[c, at], tables[t], preferred_element_type=jnp.float32)
                spread = term if spread is None else spread + term
            terms = cells[at].astype(jnp.float32) * spread
            part = jnp.sum(terms.reshape(group, depth, size), axis=0)
            total = part if total is None else total + part
        return total

    def put(dst, total):
        for m in range(groups):
            for f in range(fields):
                at = f * levels + m * share
                dst(m, slice(f * share, (f + 1) * share), total[at:at + share])

    def interior(n, carry):
        b = n + HB
        picks = [
            (b + HALF + off_s[s, b], jnp.where(s < cnt_s[0, b], tab_s[s, b], ntab))
            for s in range(nslots)
        ]
        cols = pl.ds(pl.multiple_of(n * size, size), size)

        def dst(m, at, value):
            part_in[m, at, cols] = value

        put(dst, localize(own.at[b], picks))
        return carry

    lax.fori_loop(0, nblk - 2 * HB, interior, 0)

    def to_members(src, dst, n):
        copies = []
        for d in range(1, groups):
            there = lax.rem(me + d, groups)
            copies.append(
                pltpu.make_async_remote_copy(
                    src_ref=src.at[there], dst_ref=dst.at[d - 1],
                    send_sem=rsend.at[n, d - 1], recv_sem=rrecv.at[n, d - 1],
                    device_id={"member": there}, device_id_type=MESH,
                )
            )
        for copy in copies:
            copy.start()
        return copies

    sums = [to_members(part_in, recv_in, 0)]

    chunk = 4 * size

    def static(n, carry):
        cols = pl.ds(pl.multiple_of(n * chunk, chunk), chunk)
        for f in range(fields):
            cov = cov_ref[f, 0:share]
            for m in range(1, groups):
                cov = jnp.where(me == m, cov_ref[f, m * share:(m + 1) * share], cov)
            total = cov[:, 0:1] * ctl[f * levels:f * levels + 1, cols]
            for l in range(1, levels):
                at = f * levels + l
                total = total + cov[:, l:l + 1] * ctl[at:at + 1, cols]
            out_ref[f, :, cols] = 0.5 * total
        return carry

    lax.fori_loop(0, nblk * size // chunk, static, 0)

    def away_copy(side):
        return pltpu.make_async_remote_copy(
            src_ref=away.at[side], dst_ref=back.at[1 - side],
            send_sem=asend.at[side], recv_sem=arecv.at[1 - side],
            device_id={"band": toward(side)}, device_id_type=MESH,
        )

    for phase, side in enumerate((near, far)):
        for copy in halo_copies(1 - side):
            copy.wait_recv()
        notes = [
            pltpu.make_async_copy(src.at[side], dst.at[side], side_sem.at[side, n])
            for n, (src, dst) in enumerate(
                [(off_halo, off_side), (tab_halo, tab_side), (cnt_halo, cnt_side)]
            )
        ]
        for copy in notes:
            copy.start()
        for i in range(HALF):
            words[side * (nblk + HALF) + i] = word_of(
                halo[side, i], ctl_halo[side, :, i * size:(i + 1) * size]
            )
        for copy in notes:
            copy.wait()

        for n in range(HALF):
            i = jnp.where(side == 0, n, HALF - 1 - n)
            b = jnp.where(side == 0, i, nblk + HALF + i)
            there = jnp.where(side == 0, nblk - HALF + i, i)
            picks = []
            for q in range(n + 1):
                c = jnp.where(side == 0, 2 * HALF + q, nblk - 1 - q)
                t = jnp.int32(ntab)
                for s in range(nslots):
                    hit = (off_side[side, s, there] == c - b) & (s < cnt_side[side, 0, there])
                    t = jnp.where(hit, tab_side[side, s, there], t)
                picks.append((c, t))
            cols = pl.ds(pl.multiple_of(i * size, size), size)

            def dst(m, at, value):
                away[side, m, at, cols] = value

            put(dst, localize(halo.at[side, i], picks))
        away_copy(side).start()

        def edge(n, carry):
            b = n + side * (nblk - HB)
            picks = []
            for s in range(nslots):
                c = b + HALF + off_s[s, b]
                held = (c >= 0) & (c < last) & (s < cnt_s[0, b])
                picks.append((jnp.clip(c, 0, last - 1), jnp.where(held, tab_s[s, b], ntab)))
            cols = pl.ds(pl.multiple_of(n * size, size), size)

            def dst(m, at, value):
                part_edge[side, m, at, cols] = value

            put(dst, localize(own.at[b], picks))
            return carry

        lax.fori_loop(0, HB, edge, 0)
        away_copy(1 - side).wait_recv()
        met = pl.ds(pl.multiple_of(side * HALF * size, size), HALF * size)
        part_edge[side, :, :, met] = part_edge[side, :, :, met] + back[side]
        sums.append(to_members(part_edge.at[side], recv_edge.at[side], 1 + phase))

    for side in (near, far):
        away_copy(side).wait_send()
        for copy in halo_copies(side):
            copy.wait_send()

    def finish(copies, first, width, own_part, others):
        for copy in copies:
            copy.wait()
        total = own_part
        for d in range(groups - 1):
            total = total + others[d]
        cols = pl.ds(pl.multiple_of(first * size, size), width * size)
        for f in range(fields):
            out_ref[f, :, cols] = out_ref[f, :, cols] + 0.5 * (
                total[f * share:(f + 1) * share] / scale
            )

    finish(sums[0], HB, nblk - 2 * HB, part_in[me], recv_in)
    for phase, side in enumerate((near, far)):
        finish(sums[1 + phase], side * (nblk - HB), HB, part_edge[side, me], recv_edge.at[side])


def per_device(perturb, control, static_cov, loc_table, pair_offset, pair_table, pair_count):
    groups = lax.axis_size("member")
    bands = lax.axis_size("band")
    members, fields, levels, width = perturb.shape
    ntab, size = loc_table.shape[:2]
    nblk, nslots = pair_offset.shape
    share = levels // groups
    rows = members * fields * levels
    depth = fields * levels

    offsets = pair_offset.T
    table_ids = pair_table.T
    counts = pair_count.reshape(1, nblk)
    out_rows = fields * share
    f32, bf16, i32 = jnp.float32, jnp.bfloat16, jnp.int32
    smem = pl.BlockSpec(memory_space=pltpu.SMEM)
    any_spec = pl.BlockSpec(memory_space=pl.ANY)
    dma = pltpu.SemaphoreType.DMA
    pairs = nblk * nslots
    return pl.pallas_call(
        functools.partial(
            kernel, groups, bands, nblk, size, nslots, fields, levels, ntab, members * groups - 1
        ),
        out_shape=jax.ShapeDtypeStruct((fields, share, width), f32),
        in_specs=[
            smem, smem, smem, any_spec, any_spec, any_spec, any_spec, any_spec, any_spec,
            pl.BlockSpec(memory_space=pltpu.VMEM),
        ],
        out_specs=pl.BlockSpec(memory_space=pltpu.VMEM),
        scratch_shapes=[
            pltpu.VMEM((nblk, rows, size), bf16),
            pltpu.VMEM((2, HALF, rows, size), bf16),
            pltpu.VMEM((nblk + 2 * HALF, rows, size), bf16),
            pltpu.VMEM((ntab + 1, size, size), bf16),
            pltpu.VMEM((depth, width), f32),
            pltpu.VMEM((2, depth, HALF * size), f32),
            pltpu.VMEM((2, nslots, nblk), i32),
            pltpu.VMEM((2, nslots, nblk), i32),
            pltpu.VMEM((2, 1, nblk), i32),
            pltpu.SMEM((2, nslots, nblk), i32),
            pltpu.SMEM((2, nslots, nblk), i32),
            pltpu.SMEM((2, 1, nblk), i32),
            pltpu.VMEM((groups, out_rows, width - 2 * HB * size), f32),
            pltpu.VMEM((groups - 1, out_rows, width - 2 * HB * size), f32),
            pltpu.VMEM((2, groups, out_rows, HB * size), f32),
            pltpu.VMEM((2, groups - 1, out_rows, HB * size), f32),
            pltpu.VMEM((2, groups, out_rows, HALF * size), f32),
            pltpu.VMEM((2, groups, out_rows, HALF * size), f32),
            dma((nblk,)), dma((2,)), dma((2, 3)),
            dma((2, 5)), dma((2, 5)),
            dma((2,)), dma((2,)),
            dma((3, groups - 1)), dma((3, groups - 1)),
        ],
        compiler_params=pltpu.CompilerParams(
            collective_id=0, has_side_effects=True, vmem_limit_bytes=56 * 1024 * 1024
        ),
        cost_estimate=pl.CostEstimate(
            flops=2 * pairs * rows * size * size, bytes_accessed=2 * rows * width, transcendentals=0
        ),
    )(
        offsets, table_ids, counts, offsets, table_ids, counts,
        perturb.reshape(rows, width), control.reshape(depth, width), loc_table, static_cov,
    )


def solution(mesh):
    return jax.shard_map(
        per_device,
        mesh=mesh,
        in_specs=(
            P("member", None, None, "band"),
            P(None, None, "band"),
            P(),
            P(),
            P("band", None),
            P("band", None),
            P("band"),
        ),
        out_specs=P(None, "member", "band"),
        check_vma=False,
    )
```

```python
import functools

import jax
import jax.numpy as jnp
from jax import lax
from jax.experimental import pallas as pl
from jax.experimental.pallas import tpu as pltpu
from jax.sharding import PartitionSpec as P

HB = 6
HALF = HB // 2
GROUP = 5
MESH = pl.DeviceIdType.MESH


def kernel(
    groups, bands, nblk, size, nslots, fields, levels, ntab, scale,
    off_s, tab_s, cnt_s, off_h, tab_h, cnt_h, perturb_h, control_h, table_h, cov_ref,
    out_ref,
    own, halo, words, tables, ctl, ctl_halo,
    off_halo, tab_halo, cnt_halo, off_side, tab_side, cnt_side,
    part_in, recv_in, part_edge, recv_edge, away, back,
    own_sem, misc_sem, side_sem, hsend, hrecv, asend, arecv, rsend, rrecv,
):
    rows = perturb_h.shape[0]
    depth = fields * levels
    share = levels // groups
    last = nblk + 2 * HALF
    me = lax.axis_index("member")
    mine = lax.axis_index("band")
    right = lax.rem(mine + 1, bands)
    left = lax.rem(mine + bands - 1, bands)

    barrier = pltpu.get_barrier_semaphore()
    for there in (left, right):
        pl.semaphore_signal(barrier, inc=1, device_id={"band": there}, device_id_type=MESH)
    for d in range(1, groups):
        pl.semaphore_signal(
            barrier, inc=1, device_id={"member": lax.rem(me + d, groups)}, device_id_type=MESH
        )

    def load(b):
        return pltpu.make_async_copy(
            perturb_h.at[:, pl.ds(pl.multiple_of(b * size, size), size)], own.at[b], own_sem.at[b]
        )

    def start_load(b, carry):
        load(b).start()
        return carry

    loads = [
        pltpu.make_async_copy(control_h, ctl, misc_sem.at[0]),
        pltpu.make_async_copy(table_h, tables.at[pl.ds(0, ntab)], misc_sem.at[1]),
    ]
    for copy in loads:
        copy.start()
    lax.fori_loop(0, nblk, start_load, 0)
    pl.semaphore_wait(barrier, 2 + groups - 1)

    halo_copies = []
    for side, there, first in ((0, right, nblk - HALF), (1, left, 0)):
        for n, (src, dst) in enumerate(
            [
                (off_h, off_halo.at[side]),
                (tab_h, tab_halo.at[side]),
                (cnt_h, cnt_halo.at[side]),
                (control_h.at[:, pl.ds(first * size, HALF * size)], ctl_halo.at[side]),
            ]
            + [
                (perturb_h.at[:, pl.ds((first + i) * size, size)], halo.at[side, i])
                for i in range(HALF)
            ]
        ):
            halo_copies.append(
                pltpu.make_async_remote_copy(
                    src_ref=src, dst_ref=dst, send_sem=hsend.at[side, n], recv_sem=hrecv.at[side, n],
                    device_id={"band": there}, device_id_type=MESH,
                )
            )
    for copy in halo_copies:
        copy.start()

    def word_of(block, weights):
        cells = block.astype(jnp.float32).reshape(rows // depth, depth, size) * weights[None]
        return cells.astype(jnp.bfloat16).reshape(rows, size)

    tables[ntab] = jnp.zeros((size, size), jnp.bfloat16)
    for i in range(HALF):
        words[i] = jnp.zeros((rows, size), jnp.bfloat16)
        words[nblk + HALF + i] = jnp.zeros((rows, size), jnp.bfloat16)
    for copy in loads:
        copy.wait()

    def make_words(b, carry):
        load(b).wait()
        words[b + HALF] = word_of(own[b], ctl[:, pl.ds(pl.multiple_of(b * size, size), size)])
        return carry

    lax.fori_loop(0, 2 * HB + 2, make_words, 0)

    members = rows // depth
    group = max(g for g in range(1, GROUP + 1) if members % g == 0)

    def localize(cells, picks):
        total = None
        for first in range(0, rows, group * depth):
            at = pl.ds(first, group * depth)
            spread = None
            for c, t in picks:
                term = jnp.dot(words[c, at], tables[t], preferred_element_type=jnp.float32)
                spread = term if spread is None else spread + term
            terms = cells[at].astype(jnp.float32) * spread
            part = jnp.sum(terms.reshape(group, depth, size), axis=0)
            total = part if total is None else total + part
        return total

    def put(dst, total):
        for m in range(groups):
            for f in range(fields):
                at = f * levels + m * share
                dst(m, slice(f * share, (f + 1) * share), total[at:at + share])

    def interior(n, carry):
        b = n + HB
        picks = [
            (b + HALF + off_s[s, b], jnp.where(s < cnt_s[0, b], tab_s[s, b], ntab))
            for s in range(nslots)
        ]
        cols = pl.ds(pl.multiple_of(n * size, size), size)

        def dst(m, at, value):
            part_in[m, at, cols] = value

        put(dst, localize(own.at[b], picks))
        return carry

    def two(n, carry):
        interior(2 * n, carry)
        return interior(2 * n + 1, carry)

    def two_and_words(n, carry):
        two(n, carry)
        make_words(2 * n + 2 * HB + 2, carry)
        return make_words(2 * n + 2 * HB + 3, carry)

    steps = (nblk - 2 * HB) // 2
    lax.fori_loop(0, steps - 1, two_and_words, 0)
    two(steps - 1, 0)

    def to_members(src, dst, n):
        copies = []
        for d in range(1, groups):
            there = lax.rem(me + d, groups)
            copies.append(
                pltpu.make_async_remote_copy(
                    src_ref=src.at[there], dst_ref=dst.at[d - 1],
                    send_sem=rsend.at[n, d - 1], recv_sem=rrecv.at[n, d - 1],
                    device_id={"member": there}, device_id_type=MESH,
                )
            )
        for copy in copies:
            copy.start()
        return copies

    sums = [to_members(part_in, recv_in, 0)]

    chunk = 4 * size

    def static(n, carry):
        cols = pl.ds(pl.multiple_of(n * chunk, chunk), chunk)
        for f in range(fields):
            cov = cov_ref[f, 0:share]
            for m in range(1, groups):
                cov = jnp.where(me == m, cov_ref[f, m * share:(m + 1) * share], cov)
            total = cov[:, 0:1] * ctl[f * levels:f * levels + 1, cols]
            for l in range(1, levels):
                at = f * levels + l
                total = total + cov[:, l:l + 1] * ctl[at:at + 1, cols]
            out_ref[f, :, cols] = 0.5 * total
        return carry

    lax.fori_loop(0, nblk * size // chunk, static, 0)

    for copy in halo_copies:
        copy.wait()
    sides = [
        pltpu.make_async_copy(src.at[side], dst.at[side], side_sem.at[side, n])
        for side in range(2)
        for n, (src, dst) in enumerate(
            [(off_halo, off_side), (tab_halo, tab_side), (cnt_halo, cnt_side)]
        )
    ]
    for copy in sides:
        copy.start()
    for side in range(2):
        for i in range(HALF):
            words[side * (nblk + HALF) + i] = word_of(
                halo[side, i], ctl_halo[side, :, i * size:(i + 1) * size]
            )
    for copy in sides:
        copy.wait()

    for side in range(2):
        for i in range(HALF):
            there = nblk - HALF + i if side == 0 else i
            b = i if side == 0 else nblk + HALF + i
            partners = range(2 * HALF, 2 * HALF + i + 1) if side == 0 else range(
                b - HB, nblk
            )
            picks = []
            for c in partners:
                t = jnp.int32(ntab)
                for s in range(nslots):
                    hit = (off_side[side, s, there] == c - b) & (s < cnt_side[side, 0, there])
                    t = jnp.where(hit, tab_side[side, s, there], t)
                picks.append((c, t))
            total = localize(halo.at[side, i], picks)

            def dst(m, at, value):
                away[side, m, at, i * size:(i + 1) * size] = value

            put(dst, total)
    away_copies = [
        pltpu.make_async_remote_copy(
            src_ref=away.at[side], dst_ref=back.at[1 - side],
            send_sem=asend.at[side], recv_sem=arecv.at[side],
            device_id={"band": there}, device_id_type=MESH,
        )
        for side, there in ((0, left), (1, right))
    ]
    for copy in away_copies:
        copy.start()

    for side in range(2):
        def edge(n, carry):
            b = n + side * (nblk - HB)
            picks = []
            for s in range(nslots):
                c = b + HALF + off_s[s, b]
                held = (c >= 0) & (c < last) & (s < cnt_s[0, b])
                picks.append((jnp.clip(c, 0, last - 1), jnp.where(held, tab_s[s, b], ntab)))
            cols = pl.ds(pl.multiple_of(n * size, size), size)

            def dst(m, at, value):
                part_edge[side, m, at, cols] = value

            put(dst, localize(own.at[b], picks))
            return carry

        def two_edges(n, carry):
            edge(2 * n, carry)
            return edge(2 * n + 1, carry)

        lax.fori_loop(0, HB // 2, two_edges, 0)
        if side == 0:
            for copy in away_copies:
                copy.wait()
        near = pl.ds(side * HALF * size, HALF * size)
        part_edge[side, :, :, near] = part_edge[side, :, :, near] + back[side]
        sums.append(to_members(part_edge.at[side], recv_edge.at[side], 1 + side))

    def finish(copies, first, width, own_part, others):
        for copy in copies:
            copy.wait()
        total = own_part
        for d in range(groups - 1):
            total = total + others[d]
        cols = slice(first * size, (first + width) * size)
        for f in range(fields):
            out_ref[f, :, cols] = out_ref[f, :, cols] + 0.5 * (
                total[f * share:(f + 1) * share] / scale
            )

    finish(sums[0], HB, nblk - 2 * HB, part_in[me], recv_in)
    for side in range(2):
        finish(sums[1 + side], side * (nblk - HB), HB, part_edge[side, me], recv_edge.at[side])


def per_device(perturb, control, static_cov, loc_table, pair_offset, pair_table, pair_count):
    groups = lax.axis_size("member")
    bands = lax.axis_size("band")
    members, fields, levels, width = perturb.shape
    ntab, size = loc_table.shape[:2]
    nblk, nslots = pair_offset.shape
    share = levels // groups
    rows = members * fields * levels
    depth = fields * levels

    offsets = pair_offset.T
    table_ids = pair_table.T
    counts = pair_count.reshape(1, nblk)
    out_rows = fields * share
    f32, bf16, i32 = jnp.float32, jnp.bfloat16, jnp.int32
    smem = pl.BlockSpec(memory_space=pltpu.SMEM)
    any_spec = pl.BlockSpec(memory_space=pl.ANY)
    dma = pltpu.SemaphoreType.DMA
    pairs = nblk * nslots
    return pl.pallas_call(
        functools.partial(
            kernel, groups, bands, nblk, size, nslots, fields, levels, ntab, members * groups - 1
        ),
        out_shape=jax.ShapeDtypeStruct((fields, share, width), f32),
        in_specs=[
            smem, smem, smem, any_spec, any_spec, any_spec, any_spec, any_spec, any_spec,
            pl.BlockSpec(memory_space=pltpu.VMEM),
        ],
        out_specs=pl.BlockSpec(memory_space=pltpu.VMEM),
        scratch_shapes=[
            pltpu.VMEM((nblk, rows, size), bf16),
            pltpu.VMEM((2, HALF, rows, size), bf16),
            pltpu.VMEM((nblk + 2 * HALF, rows, size), bf16),
            pltpu.VMEM((ntab + 1, size, size), bf16),
            pltpu.VMEM((depth, width), f32),
            pltpu.VMEM((2, depth, HALF * size), f32),
            pltpu.VMEM((2, nslots, nblk), i32),
            pltpu.VMEM((2, nslots, nblk), i32),
            pltpu.VMEM((2, 1, nblk), i32),
            pltpu.SMEM((2, nslots, nblk), i32),
            pltpu.SMEM((2, nslots, nblk), i32),
            pltpu.SMEM((2, 1, nblk), i32),
            pltpu.VMEM((groups, out_rows, width - 2 * HB * size), f32),
            pltpu.VMEM((groups - 1, out_rows, width - 2 * HB * size), f32),
            pltpu.VMEM((2, groups, out_rows, HB * size), f32),
            pltpu.VMEM((2, groups - 1, out_rows, HB * size), f32),
            pltpu.VMEM((2, groups, out_rows, HALF * size), f32),
            pltpu.VMEM((2, groups, out_rows, HALF * size), f32),
            dma((nblk,)), dma((2,)), dma((2, 3)),
            dma((2, 4 + HALF)), dma((2, 4 + HALF)),
            dma((2,)), dma((2,)),
            dma((3, groups - 1)), dma((3, groups - 1)),
        ],
        compiler_params=pltpu.CompilerParams(
            collective_id=0, has_side_effects=True, vmem_limit_bytes=56 * 1024 * 1024
        ),
        cost_estimate=pl.CostEstimate(
            flops=2 * pairs * rows * size * size, bytes_accessed=2 * rows * width, transcendentals=0
        ),
    )(
        offsets, table_ids, counts, offsets, table_ids, counts,
        perturb.reshape(rows, width), control.reshape(depth, width), loc_table, static_cov,
    )


def solution(mesh):
    return jax.shard_map(
        per_device,
        mesh=mesh,
        in_specs=(
            P("member", None, None, "band"),
            P(None, None, "band"),
            P(),
            P(),
            P("band", None),
            P("band", None),
            P("band"),
        ),
        out_specs=P(None, "member", "band"),
        check_vma=False,
    )
```
